256 devices in a mesh: fsdp: 16 (over x, z_hi, core), frame: 16 (over z_lo, y).
Axes of the slice: x: 4, y: 4, z: 8 (z_hi: 2, z_lo: 4; z = z_hi * 4 + z_lo), core: 2. Of those that a mesh axis runs over, the one named last changes fastest.
Arguments:
- queries: bfloat16 [32, 16, 128, 1536], P('fsdp', 'frame'), may hold values from -6 to 6
- key_vectors: bfloat16 [32, 16, 128, 1536], P('fsdp', 'frame'), may hold values from -6 to 6
- value_vectors: bfloat16 [32, 16, 128, 1536], P('fsdp', 'frame'), may hold values from -6 to 6
- out_weight: bfloat16 [1536, 1536], P(('fsdp', 'frame')), may hold values from -0.15625 to 0.15625
- grad_out: bfloat16 [32, 16, 128, 1536], P('fsdp', 'frame'), may hold values from -6 to 6
Outputs:
- projected: bfloat16 [32, 16, 128, 1536], P('fsdp', 'frame')
- grad_queries: bfloat16 [32, 16, 128, 1536], P('fsdp', 'frame')
- grad_keys: bfloat16 [32, 16, 128, 1536], P('fsdp', 'frame')
- grad_values: bfloat16 [32, 16, 128, 1536], P('fsdp', 'frame')
- grad_weight: float32 [1536, 1536], P(('fsdp', 'frame'))
The draws below stay inside these ranges and needn't reach their ends.
All inputs are finite; a program needn't handle non-finite values.
Results may differ from the reference program's by a relative error of at most 0.0058.
Values may be sent and summed in bfloat16 or wider, within the bound.
A program may use at most 128 MiB of HBM per device.

```python
import jax
import jax.numpy as jnp
from jax import lax

HEADS = 12
HEAD_SIZE = 128
OUT_WIDTH = 1536
FRAMES = 16
POSITIONS = 128
INNER = 1536
CLIPS = 32
TOKENS = 65536


def draw_queries(key, part):
    key = jax.random.fold_in(key, 1)
    values = jnp.clip(jax.random.normal(key, (CLIPS, FRAMES, POSITIONS, HEADS * HEAD_SIZE)), -6.0, 6.0)
    return values.astype(jnp.bfloat16)


def draw_key_vectors(key, part):
    key = jax.random.fold_in(key, 2)
    values = jnp.clip(jax.random.normal(key, (CLIPS, FRAMES, POSITIONS, HEADS * HEAD_SIZE)), -6.0, 6.0)
    return values.astype(jnp.bfloat16)


def block_levels(own_key, dims, cuts, smallest, largest):
    level = 1.0
    for position, shards_of in cuts:
        heights = jax.random.uniform(jax.random.fold_in(jax.random.fold_in(own_key, 6), position), (shards_of,), jnp.float32, smallest / len(cuts), largest / len(cuts))
        level = level * jnp.repeat(jnp.exp(heights), dims[position] // shards_of).reshape((-1,) + (1,) * (len(dims) - 1 - position))
    return level


def scatter_about(own_key, shape, deviation, bound, pieces=(), dtype=jnp.bfloat16):
    loudness = block_levels(own_key, shape, pieces, -0.22, 0.18) if pieces else 1.0
    entries = jax.random.normal(own_key, shape, jnp.float32) * deviation * loudness
    return jnp.minimum(jnp.maximum(entries, -bound), bound).astype(dtype)


def setup_inputs(seed: int = 0) -> dict:
    key_of = jax.random.split(jax.random.key(seed), 6)
    return {
        "queries": draw_queries(jax.random.fold_in(key_of[5], 71), 0),
        "key_vectors": draw_key_vectors(jax.random.fold_in(key_of[5], 71), 0),
        "value_vectors": scatter_about(key_of[2], (CLIPS, FRAMES, POSITIONS, INNER), 1.0, 6.0, ((0, 16), (1, 16))),
        "out_weight": scatter_about(key_of[3], (INNER, OUT_WIDTH), INNER ** -0.5, 0.15625, ((0, 256),)),
        "grad_out": scatter_about(key_of[4], (CLIPS, FRAMES, POSITIONS, OUT_WIDTH), 1.0, 6.0, ((0, 16), (1, 16))),
    }


def split_heads(block):
    return block.reshape(block.shape[:-1] + (HEADS, HEAD_SIZE))


def clip_probs(query_clip, key_clip):
    scores = jnp.einsum('fphs,gphs->phfg', split_heads(query_clip).astype(jnp.float32), split_heads(key_clip).astype(jnp.float32)) * (HEAD_SIZE ** -0.5)
    index = jnp.arange(FRAMES)
    allowed = index[:, None] >= index[None, :]
    scores = jnp.where(allowed, scores, -jnp.inf)
    return jax.nn.softmax(scores, axis=-1)


def clip_forward(inputs):
    query_clip, key_clip, value_clip = inputs
    probs = clip_probs(query_clip, key_clip)
    weights = lax.optimization_barrier(probs.astype(jnp.bfloat16))
    attended = jnp.einsum('phfg,gphs->fphs', weights.astype(jnp.float32), split_heads(value_clip).astype(jnp.float32))
    return attended.astype(jnp.bfloat16).reshape(query_clip.shape)


def clip_backward(inputs):
    query_clip, key_clip, value_clip, grad_clip = inputs
    probs = clip_probs(query_clip, key_clip)
    weights = lax.optimization_barrier(probs.astype(jnp.bfloat16)).astype(jnp.float32)
    grad_heads = split_heads(grad_clip).astype(jnp.float32)
    value_heads = split_heads(value_clip).astype(jnp.float32)
    grad_probs = jnp.einsum('fphs,gphs->phfg', grad_heads, value_heads)
    centre = jnp.sum(probs * grad_probs, axis=-1, keepdims=True)
    grad_scores = lax.optimization_barrier((probs * (grad_probs - centre)).astype(jnp.bfloat16)).astype(jnp.float32)
    factor = HEAD_SIZE ** -0.5
    grad_query = jnp.einsum('phfg,gphs->fphs', grad_scores, split_heads(key_clip).astype(jnp.float32)) * factor
    grad_key = jnp.einsum('phfg,fphs->gphs', grad_scores, split_heads(query_clip).astype(jnp.float32)) * factor
    grad_value = jnp.einsum('phfg,fphs->gphs', weights, grad_heads)
    shape = query_clip.shape
    return (grad_query.astype(jnp.bfloat16).reshape(shape), grad_key.astype(jnp.bfloat16).reshape(shape), grad_value.astype(jnp.bfloat16).reshape(shape))


def reference(queries, key_vectors, value_vectors, out_weight, grad_out):
    attended = lax.map(clip_forward, (queries, key_vectors, value_vectors))
    flat = attended.reshape(TOKENS, INNER).astype(jnp.float32)
    weight_wide = out_weight.astype(jnp.float32)
    grad_flat = grad_out.reshape(TOKENS, OUT_WIDTH).astype(jnp.float32)
    projected = jnp.dot(flat, weight_wide, precision=lax.Precision.HIGHEST).astype(jnp.bfloat16).reshape(grad_out.shape)
    grad_attended = jnp.dot(grad_flat, weight_wide.T, precision=lax.Precision.HIGHEST).astype(jnp.bfloat16).reshape(queries.shape)
    grad_weight = jnp.dot(flat.T, grad_flat, precision=lax.Precision.HIGHEST) * (TOKENS ** -0.5)
    grad_queries, grad_keys, grad_values = lax.map(clip_backward, (queries, key_vectors, value_vectors, grad_attended))
    return (projected, grad_queries, grad_keys, grad_values, grad_weight)
```

```python
import functools

import jax
import jax.numpy as jnp
from jax import lax
from jax.experimental import pallas as pl
from jax.experimental.pallas import tpu as pltpu
from jax.sharding import PartitionSpec as P

MESH = pl.DeviceIdType.MESH
F32, BF16 = jnp.float32, jnp.bfloat16
HEAD = 128
ROWS = 256
PART = 64
BAND = 16
WIDTH = 1536
LANES = 512
FACTOR = HEAD ** -0.5
TOKEN_FACTOR = 65536.0 ** -0.5
SETS = ((0, 1, 1, 1), (0, 0, 3, 3), (0, 1, 2, 2))
Q, K, V, G = range(4)
NT = (((1,), (1,)), ((), ()))
TN = (((0,), (0,)), ((), ()))


def dot(a, b, dims=(((1,), (0,)), ((), ()))):
    return lax.dot_general(a, b, dims, preferred_element_type=F32)


def query_blocks(site, where):
    return [b for b in range(4) if where[b] == site]


def key_sites(block, where):
    return [s for s in sorted(set(where)) if block <= max(query_blocks(s, where))]


def lanes_of(s):
    return pl.ds(LANES * s, LANES)


def kernel(q_in, k_in, v_in, w_in, g_in, proj_out, dq_out, dk_out, dv_out, dw_out, *refs):
    refs = list(refs)
    take = lambda n: [refs.pop(0) for _ in range(n)]
    held = [take(4) for _ in SETS]
    attended = take(len(SETS))
    g_home, o_home, ga_home, partial, proj_home = take(5)
    w_slabs, w_pad, w_full = take(3)
    dw_part, core_in, x_out, x_in, y_out, y_in, z_out, z_in = take(8)
    local_sem, in_send, in_recv, o_send, o_recv, back_send, back_recv = take(7)
    wz_send, wz_recv, wy_send, wy_recv, wx_send, wx_recv, wc_send, wc_recv = take(8)
    dc_send, dc_recv, dx_send, dx_recv, dy_send, dy_recv, dz_send, dz_recv = take(8)

    f = lax.axis_index("fsdp")
    fr = lax.axis_index("frame")
    x, zh, core = f // 4, lax.rem(f // 2, 2), lax.rem(f, 2)
    z, y = fr // 4, lax.rem(fr, 4)
    z8 = zh * 4 + z

    def z_device(d):
        t = lax.rem(z8 + d, 8)
        return {"fsdp": x * 4 + (t // 4) * 2 + core, "frame": lax.rem(t, 4) * 4 + y}

    def y_device(d):
        return {"frame": z * 4 + lax.rem(y + d, 4)}

    def x_device(d):
        return {"fsdp": lax.rem(x + d, 4) * 4 + lax.rem(f, 4)}

    other_core = {"fsdp": f + 1 - 2 * core}

    def remote(src, dst, send, recv, device):
        return pltpu.make_async_remote_copy(
            src_ref=src, dst_ref=dst, send_sem=send, recv_sem=recv, device_id=device, device_id_type=MESH
        )

    def wait_slabs(sem, n):
        ref = held[0][0].at[pl.ds(0, n)]
        pltpu.make_async_copy(ref, ref, sem).wait()

    barrier = pltpu.get_barrier_semaphore()
    for d in range(1, 16):
        pl.semaphore_signal(barrier, inc=1, device_id={"frame": lax.rem(fr + d, 16)}, device_id_type=MESH)
    for d in (1, 2, 3):
        pl.semaphore_signal(barrier, inc=1, device_id=x_device(d), device_id_type=MESH)
    pl.semaphore_signal(barrier, inc=1, device_id=other_core, device_id_type=MESH)
    for k in range(4):
        device = {"fsdp": x * 4 + (1 - zh) * 2 + core, "frame": k * 4 + y}
        pl.semaphore_signal(barrier, inc=1, device_id=device, device_id_type=MESH)
    pl.semaphore_wait(barrier, 23)

    g_load = pltpu.make_async_copy(g_in, g_home, local_sem.at[0])
    g_load.start()
    own_rows = pltpu.make_async_copy(w_in, w_slabs.at[y, z8], local_sem.at[1])
    own_rows.start()
    wz = [
        remote(w_in, w_slabs.at[y, z8], wz_send.at[d], wz_recv.at[d], z_device(d)) for d in range(1, 8)
    ]
    for c in wz:
        c.start()

    def for_each_z(fn):
        for zs in range(4):
            pl.when(z == zs)(functools.partial(fn, zs))

    sent = {}

    def send_in(zs, t, s):
        where = SETS[s]
        src = (q_in, k_in, v_in, ga_home)[t]
        sites = [where[zs]] if t in (Q, G) else key_sites(zs, where)
        count = 0
        for site in sorted(sites, key=lambda a: -abs(a - zs)):

            def part(j):
                return src.at[pl.ds(pl.multiple_of(j * PART, PART), PART), lanes_of(s)]

            def send(dy):
                j = lax.rem(y + dy, 4)
                remote(
                    part(j), held[s][t].at[fr], in_send.at[t, s], in_recv.at[t, s], {"frame": site * 4 + j}
                ).start()

            for dy in (1, 2, 3):
                send(dy)
            if site == zs:
                pltpu.make_async_copy(part(y), held[s][t].at[fr], in_recv.at[t, s]).start()
                count += 3
            else:
                send(0)
                count += 4
        sent[zs, t, s] = count

    def wait_in(zs, t, s):
        blocks = query_blocks(zs, SETS[s])
        wait_slabs(in_recv.at[t, s], 4 * len(blocks) if t in (Q, G) else 4 * (max(blocks) + 1))

    def home_rows(ref, s):
        return ref.at[pl.ds(pl.multiple_of(y * PART, PART), PART), lanes_of(s)]

    def send_home(zs, s, src, blocks, dst_of, send_sem, recv_of):
        count = 0
        for b in blocks:
            for k in (1, 2, 3, 0):
                frame = 4 * b + lax.rem(y + k, 4)
                if b == zs and k == 0:
                    pltpu.make_async_copy(src.at[frame], dst_of(b), recv_of(b)).start()
                else:
                    remote(src.at[frame], dst_of(b), send_sem, recv_of(b), {"frame": frame}).start()
                    count += 1
        return count

    def geometry(zs, s):
        blocks = query_blocks(zs, SETS[s])
        return 4 * blocks[0], 4 * (blocks[-1] + 1), 4 * (blocks[-1] + 1)

    def bias_of(first, last, keys):
        shape = ((last - first) * BAND, keys * BAND)
        row = lax.broadcasted_iota(jnp.int32, shape, 0)
        col = lax.broadcasted_iota(jnp.int32, shape, 1)
        allowed = ((row & 15) == (col & 15)) & ((row >> 4) + first >= (col >> 4))
        return jnp.where(allowed, 0.0, -jnp.inf).astype(F32)

    def probs_of(queries, keys, bias):
        scores = dot(queries, keys, NT) * FACTOR + bias
        top = jnp.max(scores, axis=1, keepdims=True)
        e = jnp.exp(scores - top)
        return e / jnp.sum(e, axis=1, keepdims=True)

    def bands(fn):
        def step(h, carry):
            lanes = pl.ds(pl.multiple_of(h * HEAD, HEAD), HEAD)
            for p in range(4):
                fn(pl.ds(p * BAND, BAND), lanes)
            return carry

        lax.fori_loop(0, 4, step, 0)

    def forward(zs, s):
        first, last, keys = geometry(zs, s)
        for t in (Q, K, V):
            wait_in(zs, t, s)
        bias = bias_of(first, last, keys)

        def band(rows, lanes):
            load = lambda t, a, b: held[s][t][a:b, rows, lanes].reshape((b - a) * BAND, HEAD)
            weights = probs_of(load(Q, first, last), load(K, 0, keys), bias).astype(BF16)
            out = dot(weights, load(V, 0, keys)).astype(BF16)
            attended[s][first:last, rows, lanes] = out.reshape(last - first, BAND, HEAD)

        bands(band)
        sent[zs, "o", s] = send_home(
            zs, s, attended[s], query_blocks(zs, SETS[s]), lambda b: home_rows(o_home, s), o_send.at[s],
            lambda b: o_recv.at[s],
        )

    def backward(zs, s):
        first, last, keys = geometry(zs, s)
        wait_in(zs, G, s)
        bias = bias_of(first, last, keys)

        def band(rows, lanes):
            load = lambda t, a, b: held[s][t][a:b, rows, lanes].reshape((b - a) * BAND, HEAD)
            queries, keys_, values, grads = load(Q, first, last), load(K, 0, keys), load(V, 0, keys), load(G, first, last)
            probs = probs_of(queries, keys_, bias)
            grad_probs = dot(grads, values, NT)
            centre = jnp.sum(probs * grad_probs, axis=1, keepdims=True)
            grad_scores = (probs * (grad_probs - centre)).astype(BF16)
            weights = probs.astype(BF16)
            grad_q = (dot(grad_scores, keys_) * FACTOR).astype(BF16)
            grad_k = (dot(grad_scores, queries, TN) * FACTOR).astype(BF16)
            grad_v = dot(weights, grads, TN).astype(BF16)
            held[s][Q][first:last, rows, lanes] = grad_q.reshape(last - first, BAND, HEAD)
            held[s][K][0:keys, rows, lanes] = grad_k.reshape(keys, BAND, HEAD)
            held[s][V][0:keys, rows, lanes] = grad_v.reshape(keys, BAND, HEAD)

        bands(band)
        sent[zs, "q", s] = send_home(
            zs, s, held[s][Q], query_blocks(zs, SETS[s]), lambda b: home_rows(dq_out, s), back_send.at[0, s],
            lambda b: back_recv.at[0, s, 0],
        )
        for t, out in ((K, dk_out), (V, dv_out)):

            def dst_of(b, t=t, out=out):
                sites = key_sites(b, SETS[s])
                ref = out if len(sites) == 1 else partial.at[t - K, sites.index(zs)]
                return home_rows(ref, s)

            sent[zs, ("k", "v")[t - K], s] = send_home(
                zs, s, held[s][t], range(keys // 4), dst_of, back_send.at[t, s],
                lambda b, t=t: back_recv.at[t, s, key_sites(b, SETS[s]).index(zs)],
            )

    def each_set(fn):
        def at(zs):
            for s in range(len(SETS)):
                if zs in SETS[s]:
                    fn(zs, s)

        for_each_z(at)

    def send_qkv(s):
        for_each_z(lambda zs: [send_in(zs, t, s) for t in (Q, K, V)] and None)

    def at_sites(fn, s):
        for zs in sorted(set(SETS[s])):
            pl.when(z == zs)(functools.partial(fn, zs, s))

    send_qkv(0)

    for c in wz:
        c.wait()
    own_rows.wait()
    wy = [
        remote(w_slabs.at[y], w_slabs.at[y], wy_send.at[d], wy_recv.at[d], y_device(d)) for d in (1, 2, 3)
    ]
    for c in wy:
        c.start()

    send_qkv(1)
    send_qkv(2)

    w_pad[...] = jnp.zeros_like(w_pad)
    r = lax.broadcasted_iota(jnp.int32, (96, 128), 0)
    c_ = lax.broadcasted_iota(jnp.int32, (96, 128), 1)
    sixth = (r * 171) >> 10
    pick = jnp.where(c_ == r + 2 * sixth, 1.0, 0.0).astype(BF16)
    for c in wy:
        c.wait()

    def w_rows(xx, h, cc):
        return w_full.at[pl.ds(pl.multiple_of((4 * xx + 2 * h + cc) * 96, 96), 96)]

    def x_from(d):
        return lax.rem(x + 4 - d, 4)

    def core_copy(d, h):
        return remote(w_rows(x_from(d), h, core), w_rows(x_from(d), h, core), wc_send.at[d, h], wc_recv.at[d, h], other_core)

    wx = {}
    for h in range(2):
        for i in range(16):
            w_pad[8 * i : 8 * i + 6, :] = w_slabs[i % 4, 4 * h + i // 4].astype(F32)
        w_rows(x, h, core)[...] = dot(pick, w_pad[...].astype(BF16)).astype(BF16)
        for d in (1, 2, 3):
            wx[d, h] = remote(w_rows(x, h, core), w_rows(x, h, core), wx_send.at[d, h], wx_recv.at[d, h], x_device(d))
            wx[d, h].start()
        core_copy(0, h).start()

    at_sites(forward, 0)

    for d in (1, 2, 3):
        for h in range(2):
            wx[d, h].wait()
            core_copy(d, h).start()

    at_sites(forward, 1)
    at_sites(forward, 2)

    for d in range(4):
        for h in range(2):
            core_copy(d, h).wait()
    g_load.wait()
    for s in range(len(SETS)):
        ga_home[:, lanes_of(s)] = dot(g_home[...], w_full[LANES * s : LANES * (s + 1), :], NT).astype(BF16)
        for_each_z(lambda zs: send_in(zs, G, s))

    for s in range(len(SETS)):
        wait_slabs(o_recv.at[s], 4)

    def dw_rows(xx, h, cc):
        return pl.ds(pl.multiple_of((4 * xx + 2 * h + cc) * 96, 96), 96)

    dc = {}
    for d in (1, 2, 3, 0):
        xx = lax.rem(x + d, 4)
        block = pl.ds(pl.multiple_of(xx * 384, 384), 384)
        left = o_home[:, block]
        for n in range(3):
            cols = pl.ds(n * LANES, LANES)
            dw_part[block, cols] = (dot(left, g_home[:, cols], TN) * TOKEN_FACTOR).astype(BF16)
        for h in range(2):
            dc[d, h] = remote(
                dw_part.at[dw_rows(xx, h, 1 - core)], core_in.at[d, h], dc_send.at[d, h], dc_recv.at[d, h], other_core
            )
            dc[d, h].start()

    at_sites(backward, 0)

    dx = {}
    for d in (1, 2, 3, 0):
        xx = lax.rem(x + d, 4)
        for h in range(2):
            dc[d, h].wait()
            x_out[d, h * 96 : (h + 1) * 96, :] = (
                dw_part[dw_rows(xx, h, core), :].astype(F32) + core_in[d, h].astype(F32)
            ).astype(BF16)
        if d:
            dx[d] = remote(x_out.at[d], x_in.at[d], dx_send.at[d], dx_recv.at[d], x_device(d))
            dx[d].start()

    at_sites(backward, 1)
    at_sites(backward, 2)

    for n in range(3):
        cols = pl.ds(n * LANES, LANES)
        proj_home[:, cols] = dot(o_home[...], w_full[:, cols]).astype(BF16)
    proj_copy = pltpu.make_async_copy(proj_home, proj_out, local_sem.at[2])
    proj_copy.start()

    for d in (1, 2, 3):
        dx[d].wait()
    r = lax.broadcasted_iota(jnp.int32, (192, 192), 0)
    c_ = lax.broadcasted_iota(jnp.int32, (192, 192), 1)
    slab = (r * 171) >> 10
    source = 24 * (slab & 7) + 6 * (slab >> 3) + (r - 6 * slab)
    order = jnp.where(c_ == source, 1.0, 0.0).astype(BF16)
    for n in range(3):
        cols = pl.ds(n * LANES, LANES)
        total = x_out[0, :, cols].astype(F32)
        for d in (1, 2, 3):
            total += x_in[d, :, cols].astype(F32)
        y_out[:, :, cols] = dot(order, total.astype(BF16)).astype(BF16).reshape(4, 48, LANES)
    dy = {}
    for d in (1, 2, 3):
        dy[d] = remote(y_out.at[lax.rem(y + d, 4)], y_in.at[d], dy_send.at[d], dy_recv.at[d], y_device(d))
        dy[d].start()
    for d in (1, 2, 3):
        dy[d].wait()
    r = lax.broadcasted_iota(jnp.int32, (64, 48), 0)
    c_ = lax.broadcasted_iota(jnp.int32, (64, 48), 1)
    spread = jnp.where((c_ == r - 2 * (r >> 3)) & ((r & 7) < 6), 1.0, 0.0).astype(BF16)
    total = y_out[y].astype(F32)
    for d in (1, 2, 3):
        total += y_in[d].astype(F32)
    slabs = dot(spread, total.astype(BF16))
    for i in range(8):
        z_out[i] = slabs[8 * i : 8 * i + 6].astype(BF16)
    dz = {}
    for d in range(1, 8):
        dz[d] = remote(z_out.at[lax.rem(z8 + d, 8)], z_in.at[d], dz_send.at[d], dz_recv.at[d], z_device(d))
        dz[d].start()

    def finish(zs):
        for s in range(len(SETS)):
            n = len(key_sites(zs, SETS[s]))
            for t, out in ((K, dk_out), (V, dv_out)):
                for site in range(n):
                    wait_slabs(back_recv.at[t, s, site], 4)
                if n > 1:
                    terms = partial.at[t - K]

                    def add(i, carry, terms=terms, n=n, s=s):
                        rows = pl.ds(pl.multiple_of(i * PART, PART), PART)
                        total = terms[0, rows, lanes_of(s)].astype(F32)
                        for site in range(1, n):
                            total += terms[site, rows, lanes_of(s)].astype(F32)
                        terms[0, rows, lanes_of(s)] = total.astype(BF16)
                        return carry

                    lax.fori_loop(0, ROWS // PART, add, 0)
                    pltpu.make_async_copy(
                        terms.at[0, :, lanes_of(s)], out.at[:, lanes_of(s)], back_recv.at[t, s, 0]
                    ).start()
            wait_slabs(back_recv.at[0, s, 0], 4)

    for_each_z(finish)

    for d in range(1, 8):
        dz[d].wait()
    total = z_out[z8].astype(F32)
    for d in range(1, 8):
        total += z_in[d].astype(F32)
    dw_out[...] = total

    proj_copy.wait()

    def drain(zs):
        for s in range(len(SETS)):
            if len(key_sites(zs, SETS[s])) > 1:
                for t in (K, V):
                    wait_slabs(back_recv.at[t, s, 0], 4)
            for t in range(4):
                wait_slabs(in_send.at[t, s], sent[zs, t, s])
            if zs in SETS[s]:
                wait_slabs(o_send.at[s], sent[zs, "o", s])
                for t in range(3):
                    wait_slabs(back_send.at[t, s], sent[zs, "qkv"[t], s])

    for_each_z(drain)


def local(queries, key_vectors, value_vectors, out_weight, grad_out):
    shape = queries.shape
    flat = lambda a: a.reshape(ROWS, WIDTH)
    any_, vmem = pl.BlockSpec(memory_space=pl.ANY), pl.BlockSpec(memory_space=pltpu.VMEM)
    dma = lambda *n: pltpu.SemaphoreType.DMA(n)
    n = len(SETS)
    big = jax.ShapeDtypeStruct((ROWS, WIDTH), BF16)
    scratch = [pltpu.VMEM((16, PART, LANES), BF16)] * (5 * n)
    scratch += [pltpu.VMEM((ROWS, WIDTH), BF16)] * 3 + [pltpu.VMEM((2, 3, ROWS, WIDTH), BF16), pltpu.VMEM((ROWS, WIDTH), BF16)]
    scratch += [pltpu.VMEM((4, 8, 6, WIDTH), BF16), pltpu.VMEM((128, WIDTH), F32), pltpu.VMEM((WIDTH, WIDTH), BF16)]
    scratch += [
        pltpu.VMEM((WIDTH, WIDTH), BF16),
        pltpu.VMEM((4, 2, 96, WIDTH), BF16),
        pltpu.VMEM((4, 192, WIDTH), BF16),
        pltpu.VMEM((4, 192, WIDTH), BF16),
        pltpu.VMEM((4, 48, WIDTH), BF16),
        pltpu.VMEM((4, 48, WIDTH), BF16),
        pltpu.VMEM((8, 6, WIDTH), BF16),
        pltpu.VMEM((8, 6, WIDTH), BF16),
    ]
    scratch += [dma(3), dma(4, n), dma(4, n), dma(n), dma(n), dma(3, n), dma(3, n, 3)]
    scratch += [dma(8), dma(8), dma(4), dma(4), dma(4, 2), dma(4, 2), dma(4, 2), dma(4, 2)]
    scratch += [dma(4, 2), dma(4, 2), dma(4), dma(4), dma(4), dma(4), dma(8), dma(8)]
    proj, dq, dk, dv, dw = pl.pallas_call(
        kernel,
        out_shape=[big] * 4 + [jax.ShapeDtypeStruct((6, WIDTH), F32)],
        in_specs=[any_] * 5,
        out_specs=[any_] * 4 + [vmem],
        scratch_shapes=scratch,
        compiler_params=pltpu.CompilerParams(
            collective_id=0, has_side_effects=True, vmem_limit_bytes=63 * 2**20
        ),
    )(flat(queries), flat(key_vectors), flat(value_vectors), out_weight, flat(grad_out))
    return tuple(a.reshape(shape) for a in (proj, dq, dk, dv)) + (dw,)


def solution(mesh):
    tokens, rows = P("fsdp", "frame", None, None), P(("fsdp", "frame"), None)
    return jax.shard_map(
        local,
        mesh=mesh,
        in_specs=(tokens, tokens, tokens, rows, tokens),
        out_specs=(tokens, tokens, tokens, tokens, rows),
        check_vma=False,
    )
```

```python
import functools

import jax
import jax.numpy as jnp
from jax import lax
from jax.experimental import pallas as pl
from jax.experimental.pallas import tpu as pltpu
from jax.sharding import PartitionSpec as P

MESH = pl.DeviceIdType.MESH
F32, BF16 = jnp.float32, jnp.bfloat16
HEAD = 128
ROWS = 256
PART = 64
BAND = 16
WIDTH = 1536
LANES = 512
FACTOR = HEAD ** -0.5
TOKEN_FACTOR = 65536.0 ** -0.5
SETS = ((1, 1, 1, 1), (0, 0, 2, 2), (0, 0, 3, 3))
Q, K, V, G = range(4)
NT = (((1,), (1,)), ((), ()))
TN = (((0,), (0,)), ((), ()))


def dot(a, b, dims=(((1,), (0,)), ((), ()))):
    return lax.dot_general(a, b, dims, preferred_element_type=F32)


def query_blocks(site, where):
    return [b for b in range(4) if where[b] == site]


def key_sites(block, where):
    return [s for s in sorted(set(where)) if block <= max(query_blocks(s, where))]


def lanes_of(s):
    return pl.ds(LANES * s, LANES)


def kernel(q_in, k_in, v_in, w_in, g_in, proj_out, dq_out, dk_out, dv_out, dw_out, *refs):
    refs = list(refs)
    take = lambda n: [refs.pop(0) for _ in range(n)]
    held = [take(4) for _ in SETS]
    attended = take(len(SETS))
    (partial,) = take(1)
    g_home, o_home, ga_home, proj_home = take(4)
    w_slabs, w_pad, w_full = take(3)
    x_own, x_out, x_in, y_out, y_in, z_out, z_in = take(7)
    local_sem, in_send, iy_recv, iz_recv, o_send, o_recv, by_send, home_recv = take(8)
    wz_send, wz_recv, wy_send, wy_recv, wx_send, wx_recv, wc_send, wc_recv = take(8)
    gc_send, gc_recv, oc_send, oc_recv, dx_send, dx_recv, dy_send, dy_recv, dz_send, dz_recv = take(10)

    f = lax.axis_index("fsdp")
    fr = lax.axis_index("frame")
    x, zh, core = f // 4, lax.rem(f // 2, 2), lax.rem(f, 2)
    z, y = fr // 4, lax.rem(fr, 4)
    z8 = zh * 4 + z

    def z_device(d):
        t = lax.rem(z8 + d, 8)
        return {"fsdp": x * 4 + (t // 4) * 2 + core, "frame": lax.rem(t, 4) * 4 + y}

    def y_device(d):
        return {"frame": z * 4 + lax.rem(y + d, 4)}

    def x_device(d):
        return {"fsdp": lax.rem(x + d, 4) * 4 + lax.rem(f, 4)}

    other_core = {"fsdp": f + 1 - 2 * core}

    def remote(src, dst, send, recv, device):
        return pltpu.make_async_remote_copy(
            src_ref=src, dst_ref=dst, send_sem=send, recv_sem=recv, device_id=device, device_id_type=MESH
        )

    def wait_slabs(sem, n):
        if n:
            ref = held[0][0].at[pl.ds(0, n)]
            pltpu.make_async_copy(ref, ref, sem).wait()

    barrier = pltpu.get_barrier_semaphore()
    partners = [{"frame": lax.rem(fr + d, 16)} for d in range(1, 16)]
    partners += [{"fsdp": x * 4 + (1 - zh) * 2 + core, "frame": k * 4 + y} for k in range(4)]
    partners += [x_device(d) for d in (1, 2, 3)] + [other_core]
    for device in partners:
        pl.semaphore_signal(barrier, inc=1, device_id=device, device_id_type=MESH)
    pl.semaphore_wait(barrier, len(partners))

    g_load = pltpu.make_async_copy(g_in, g_home.at[0], local_sem.at[0])
    g_load.start()
    own_rows = pltpu.make_async_copy(w_in, w_slabs.at[y, z8], local_sem.at[1])
    own_rows.start()
    wz = [
        remote(w_in, w_slabs.at[y, z8], wz_send.at[d], wz_recv.at[d], z_device(d)) for d in range(1, 8)
    ]
    for c in wz:
        c.start()

    def at(places, fn, *args):
        for zs in places:
            pl.when(z == zs)(functools.partial(fn, zs, *args))

    every = range(4)
    sent = {}

    def part(ref, j, s):
        return ref.at[pl.ds(pl.multiple_of(j * PART, PART), PART), lanes_of(s)]

    def own(ref, zs):
        return ref.at[pl.ds(4 * zs, 4)]

    def sites_for(b, t, s):
        return [SETS[s][b]] if t in (Q, G) else key_sites(b, SETS[s])

    def others(b, t, s):
        return sorted((a for a in sites_for(b, t, s) if a != b), key=lambda a: -abs(a - b))

    def send_in(zs, t, s):
        src = (q_in, k_in, v_in, ga_home)[t]
        count = 0
        for site in others(zs, t, s) + [zs]:
            if site not in sites_for(zs, t, s):
                continue
            recv = (iy_recv if site == zs else iz_recv).at[t, s]
            for d in (2, 1, 3, 0):
                j = lax.rem(y + d, 4)
                if site == zs and d == 0:
                    pltpu.make_async_copy(part(src, j, s), held[s][t].at[fr], recv).start()
                else:
                    device = {"frame": site * 4 + j}
                    remote(part(src, j, s), held[s][t].at[fr], in_send.at[t, s], recv, device).start()
                    count += 1
        sent["in", zs, t, s] = count

    def wait_in(zs, t, s):
        blocks = query_blocks(zs, SETS[s])
        wait_slabs(iy_recv.at[t, s], 4)
        wait_slabs(iz_recv.at[t, s], 4 * (len(blocks) - 1) if t in (Q, G) else 4 * max(blocks))

    def home(zs, s, b, src, dst, send_sem, recv_sem):
        for d in (2, 1, 3, 0):
            frame = 4 * b + lax.rem(y + d, 4)
            if b == zs and d == 0:
                pltpu.make_async_copy(src.at[frame], dst, recv_sem).start()
            else:
                remote(src.at[frame], dst, send_sem, recv_sem, {"frame": frame}).start()
        return 3 if b == zs else 4

    def geometry(zs, s):
        blocks = query_blocks(zs, SETS[s])
        return 4 * blocks[0], 4 * (blocks[-1] + 1), 4 * (blocks[-1] + 1)

    def bias_of(first, last, keys):
        shape = ((last - first) * BAND, keys * BAND)
        row = lax.broadcasted_iota(jnp.int32, shape, 0)
        col = lax.broadcasted_iota(jnp.int32, shape, 1)
        allowed = ((row & 15) == (col & 15)) & ((row >> 4) + first >= (col >> 4))
        return jnp.where(allowed, 0.0, -jnp.inf).astype(F32)

    def probs_of(queries, keys, bias):
        scores = [dot(a, b, NT) * FACTOR + bias for a, b in zip(queries, keys)]
        top = [jnp.max(a, axis=1, keepdims=True) for a in scores]
        e = [jnp.exp(a - b) for a, b in zip(scores, top)]
        scale = [1.0 / jnp.sum(a, axis=1, keepdims=True) for a in e]
        return [a * b for a, b in zip(e, scale)]

    def heads(fn):
        def step(h, carry):
            fn(pl.ds(pl.multiple_of(h * HEAD, HEAD), HEAD))
            return carry

        lax.fori_loop(0, 4, step, 0)

    bands = [pl.ds(p * BAND, BAND) for p in range(4)]

    def load(ref, a, b, lanes):
        return [ref[a:b, rows, lanes].reshape((b - a) * BAND, HEAD) for rows in bands]

    def store(ref, a, b, lanes, values):
        for rows, value in zip(bands, values):
            ref[a:b, rows, lanes] = value.astype(BF16).reshape(b - a, BAND, HEAD)

    def forward(zs, s):
        first, last, keys = geometry(zs, s)
        for t in (K, V, Q):
            wait_in(zs, t, s)
        bias = bias_of(first, last, keys)

        def head(lanes):
            queries, keys_ = load(held[s][Q], first, last, lanes), load(held[s][K], 0, keys, lanes)
            values = load(held[s][V], 0, keys, lanes)
            weights = [a.astype(BF16) for a in probs_of(queries, keys_, bias)]
            store(attended[s], first, last, lanes, [dot(a, b) for a, b in zip(weights, values)])

        heads(head)
        sent["o", zs, 0, s] = sum(
            home(zs, s, b, attended[s], part(o_home.at[0], y, s), o_send.at[s], o_recv.at[s])
            for b in sorted(query_blocks(zs, SETS[s]), key=lambda b: -abs(b - zs))
        )

    def backward(zs, s):
        first, last, keys = geometry(zs, s)
        wait_in(zs, G, s)
        bias = bias_of(first, last, keys)

        def head(lanes):
            queries, keys_ = load(held[s][Q], first, last, lanes), load(held[s][K], 0, keys, lanes)
            values, grads = load(held[s][V], 0, keys, lanes), load(held[s][G], first, last, lanes)
            grad_probs = [dot(a, b, NT) for a, b in zip(grads, values)]
            probs = probs_of(queries, keys_, bias)
            centre = [jnp.sum(a * b, axis=1, keepdims=True) for a, b in zip(probs, grad_probs)]
            grad_scores = [(a * (b - c)).astype(BF16) for a, b, c in zip(probs, grad_probs, centre)]
            weights = [a.astype(BF16) for a in probs]
            grad_q = [dot(a, b) * FACTOR for a, b in zip(grad_scores, keys_)]
            grad_k = [dot(a, b, TN) * FACTOR for a, b in zip(grad_scores, queries)]
            grad_v = [dot(a, b, TN) for a, b in zip(weights, grads)]
            store(held[s][Q], first, last, lanes, grad_q)
            store(held[s][K], 0, keys, lanes, grad_k)
            store(held[s][V], 0, keys, lanes, grad_v)

        heads(head)
        for t in (K, V, Q):
            blocks = query_blocks(zs, SETS[s]) if t == Q else range(keys // 4)
            count = 0
            for b in sorted(blocks, key=lambda b: -abs(b - zs)):
                sites = sites_for(b, t, s)
                slot = sites.index(zs)
                dst = (dq_out, dk_out, dv_out)[t]
                dst = part(dst, y, s) if len(sites) == 1 else part(partial.at[t - K, s, slot], y, 0)
                count += home(zs, s, b, held[s][t], dst, by_send.at[t, s], home_recv.at[t, s, slot])
            sent["back", zs, t, s] = count

    def arrived(zs, t, s):
        n = len(sites_for(zs, t, s))
        for slot in range(n):
            wait_slabs(home_recv.at[t, s, slot], 4)
        if n > 1:
            terms = partial.at[t - K, s]

            def add(i, carry):
                rows = pl.ds(pl.multiple_of(i * PART, PART), PART)
                total = terms[0, rows, :].astype(F32)
                for slot in range(1, n):
                    total += terms[slot, rows, :].astype(F32)
                terms[0, rows, :] = total.astype(BF16)
                return carry

            lax.fori_loop(0, ROWS // PART, add, 0)
            dst = (dq_out, dk_out, dv_out)[t]
            pltpu.make_async_copy(terms.at[0], dst.at[:, lanes_of(s)], home_recv.at[t, s, 0]).start()

    def stored(zs, t, s):
        if len(sites_for(zs, t, s)) > 1:
            wait_slabs(home_recv.at[t, s, 0], 4)

    def sites_of(s):
        return sorted(set(SETS[s]))

    g_other = remote(g_in, g_home.at[1], gc_send.at[0], gc_recv.at[0], other_core)
    g_other.start()
    for c in wz:
        c.wait()
    own_rows.wait()
    wy = [
        remote(w_slabs.at[y], w_slabs.at[y], wy_send.at[d], wy_recv.at[d], y_device(d)) for d in (1, 2, 3)
    ]
    for c in wy:
        c.start()

    for s in range(len(SETS)):
        for t in (K, V, Q):
            at(every, send_in, t, s)

    w_pad[...] = jnp.zeros_like(w_pad)
    r = lax.broadcasted_iota(jnp.int32, (96, 128), 0)
    c_ = lax.broadcasted_iota(jnp.int32, (96, 128), 1)
    sixth = (r * 171) >> 10
    pick = jnp.where(c_ == r + 2 * sixth, 1.0, 0.0).astype(BF16)
    for c in wy:
        c.wait()

    def w_rows(xx, h, cc):
        return w_full.at[pl.ds(pl.multiple_of((4 * xx + 2 * h + cc) * 96, 96), 96)]

    def x_from(d):
        return lax.rem(x + 4 - d, 4)

    def core_copy(d, h):
        ref = w_rows(x_from(d), h, core)
        return remote(ref, ref, wc_send.at[d, h], wc_recv.at[d, h], other_core)

    wx = {}
    for h in range(2):
        for i in range(16):
            w_pad[8 * i : 8 * i + 6, :] = w_slabs[i % 4, 4 * h + i // 4].astype(F32)
        w_rows(x, h, core)[...] = dot(pick, w_pad[...].astype(BF16)).astype(BF16)
        for d in (1, 3):
            wx[d, h] = remote(w_rows(x, h, core), w_rows(x, h, core), wx_send.at[d, h], wx_recv.at[d, h], x_device(d))
            wx[d, h].start()
        core_copy(0, h).start()
    for h in range(2):
        wx[2, h] = remote(w_rows(x, h, core), w_rows(x, h, core), wx_send.at[2, h], wx_recv.at[2, h], x_device(2))
        wx[2, h].start()

    at(sites_of(0), forward, 0)
    at(sites_of(1), forward, 1)

    def pass_on(d):
        for h in range(2):
            wx[d, h].wait()
            core_copy(d, h).start()

    pass_on(1)
    pass_on(3)
    at(sites_of(2), forward, 2)
    pass_on(2)

    for d in range(4):
        for h in range(2):
            core_copy(d, h).wait()
    g_load.wait()
    for s in range(len(SETS)):
        ga_home[:, lanes_of(s)] = dot(g_home[0], w_full[LANES * s : LANES * (s + 1), :], NT).astype(BF16)
        at(every, send_in, G, s)

    o_other = []
    for s in range(len(SETS)):
        wait_slabs(o_recv.at[s], 4)
        c = remote(
            o_home.at[0, :, lanes_of(s)], o_home.at[1, :, lanes_of(s)], oc_send.at[s], oc_recv.at[s], other_core
        )
        c.start()
        o_other.append(c)

    g_other.wait()
    for c in o_other:
        c.wait()
    r = lax.broadcasted_iota(jnp.int32, (384, 192), 0)
    c_ = lax.broadcasted_iota(jnp.int32, (384, 192), 1)
    side = jnp.where(r == c_ + 96 * core + jnp.where(c_ >= 96, 96, 0), 1.0, 0.0).astype(BF16)
    dx = {}
    for d in (2, 1, 3, 0):
        block = pl.ds(pl.multiple_of(lax.rem(x + d, 4) * 384, 384), 384)
        left = dot(o_home[:, :, block].reshape(2 * ROWS, 384), side).astype(BF16)
        for n in range(3):
            cols = pl.ds(n * LANES, LANES)
            term = dot(left, g_home[:, :, cols].reshape(2 * ROWS, LANES), TN) * TOKEN_FACTOR
            if d:
                x_out[d, :, cols] = term.astype(BF16)
            else:
                x_own[:, cols] = term
        if d:
            dx[d] = remote(x_out.at[d], x_in.at[d], dx_send.at[d], dx_recv.at[d], x_device(d))
            dx[d].start()

    for s in range(len(SETS)):
        at(sites_of(s), backward, s)

    for n in range(3):
        cols = pl.ds(n * LANES, LANES)
        proj_home[:, cols] = dot(o_home[0], w_full[:, cols]).astype(BF16)
    proj_copy = pltpu.make_async_copy(proj_home, proj_out, local_sem.at[2])
    proj_copy.start()

    for d in (1, 2, 3):
        dx[d].wait()
    r = lax.broadcasted_iota(jnp.int32, (192, 192), 0)
    c_ = lax.broadcasted_iota(jnp.int32, (192, 192), 1)
    slab = (r * 171) >> 10
    source = 24 * (slab & 7) + 6 * (slab >> 3) + (r - 6 * slab)
    order = jnp.where(c_ == source, 1.0, 0.0).astype(BF16)
    for n in range(3):
        cols = pl.ds(n * LANES, LANES)
        total = x_own[:, cols]
        for d in (1, 2, 3):
            total += x_in[d, :, cols].astype(F32)
        y_out[:, :, cols] = dot(order, total.astype(BF16)).astype(BF16).reshape(4, 48, LANES)
    dy = {}
    for d in (1, 2, 3):
        dy[d] = remote(y_out.at[lax.rem(y + d, 4)], y_in.at[d], dy_send.at[d], dy_recv.at[d], y_device(d))
        dy[d].start()

    for d in (1, 2, 3):
        dy[d].wait()
    r = lax.broadcasted_iota(jnp.int32, (64, 48), 0)
    c_ = lax.broadcasted_iota(jnp.int32, (64, 48), 1)
    apart = jnp.where((c_ == r - 2 * (r >> 3)) & ((r & 7) < 6), 1.0, 0.0).astype(BF16)
    total = y_out[y].astype(F32)
    for d in (1, 2, 3):
        total += y_in[d].astype(F32)
    slabs = dot(apart, total.astype(BF16))
    for i in range(8):
        z_out[i] = slabs[8 * i : 8 * i + 6].astype(BF16)
    dz = {}
    for d in range(1, 8):
        dz[d] = remote(z_out.at[lax.rem(z8 + d, 8)], z_in.at[d], dz_send.at[d], dz_recv.at[d], z_device(d))
        dz[d].start()

    for s in range(len(SETS)):
        for t in (K, V, Q):
            at(every, arrived, t, s)

    for d in range(1, 8):
        dz[d].wait()
    total = z_out[z8].astype(F32)
    for d in range(1, 8):
        total += z_in[d].astype(F32)
    dw_out[...] = total

    proj_copy.wait()

    def drain(zs):
        for s in range(len(SETS)):
            for t in range(4):
                wait_slabs(in_send.at[t, s], sent["in", zs, t, s])
            for t in (K, V, Q):
                stored(zs, t, s)
            if zs in SETS[s]:
                wait_slabs(o_send.at[s], sent["o", zs, 0, s])
                for t in (K, V, Q):
                    wait_slabs(by_send.at[t, s], sent["back", zs, t, s])

    at(every, drain)


def hand_on(*refs):
    n = len(refs) // 3
    sources, results, held, sem = refs[:n], refs[n : 2 * n], refs[2 * n : 3 * n], refs[3 * n]
    loads = [pltpu.make_async_copy(a, b, sem.at[i]) for i, (a, b) in enumerate(zip(sources, held))]
    stores = [pltpu.make_async_copy(a, b, sem.at[i]) for i, (a, b) in enumerate(zip(held, results))]
    for c in loads:
        c.start()
    for c, d in zip(loads, stores):
        c.wait()
        d.start()
    for c in stores:
        c.wait()


def local(queries, key_vectors, value_vectors, out_weight, grad_out):
    shape = queries.shape
    flat = lambda a: a.reshape(ROWS, WIDTH)
    any_, vmem = pl.BlockSpec(memory_space=pl.ANY), pl.BlockSpec(memory_space=pltpu.VMEM)
    dma = lambda *n: pltpu.SemaphoreType.DMA(n)
    n = len(SETS)
    big = jax.ShapeDtypeStruct((ROWS, WIDTH), BF16)
    scratch = [pltpu.VMEM((16, PART, LANES), BF16)] * (5 * n)
    scratch += [pltpu.VMEM((2, n, 2, ROWS, LANES), BF16)]
    scratch += [pltpu.VMEM((2, ROWS, WIDTH), BF16)] * 2 + [pltpu.VMEM((ROWS, WIDTH), BF16)] * 2
    scratch += [pltpu.VMEM((4, 8, 6, WIDTH), BF16), pltpu.VMEM((128, WIDTH), F32), pltpu.VMEM((WIDTH, WIDTH), BF16)]
    scratch += [
        pltpu.VMEM((192, WIDTH), F32),
        pltpu.VMEM((4, 192, WIDTH), BF16),
        pltpu.VMEM((4, 192, WIDTH), BF16),
        pltpu.VMEM((4, 48, WIDTH), BF16),
        pltpu.VMEM((4, 48, WIDTH), BF16),
        pltpu.VMEM((8, 6, WIDTH), BF16),
        pltpu.VMEM((8, 6, WIDTH), BF16),
    ]
    scratch += [dma(3), dma(4, n), dma(4, n), dma(4, n)]
    scratch += [dma(n), dma(n), dma(3, n), dma(3, n, 2)]
    scratch += [dma(8), dma(8), dma(4), dma(4), dma(4, 2), dma(4, 2), dma(4, 2), dma(4, 2)]
    scratch += [dma(1), dma(1), dma(n), dma(n), dma(4), dma(4), dma(4), dma(4), dma(8), dma(8)]
    proj, dq, dk, dv, dw = pl.pallas_call(
        kernel,
        out_shape=[big] * 4 + [jax.ShapeDtypeStruct((6, WIDTH), F32)],
        in_specs=[any_] * 5,
        out_specs=[any_] * 4 + [vmem],
        scratch_shapes=scratch,
        compiler_params=pltpu.CompilerParams(
            collective_id=0, has_side_effects=True, vmem_limit_bytes=63 * 2**20
        ),
    )(flat(queries), flat(key_vectors), flat(value_vectors), out_weight, flat(grad_out))
    results = (proj, dq, dk, dv, dw)
    proj, dq, dk, dv, dw = pl.pallas_call(
        hand_on,
        out_shape=[jax.ShapeDtypeStruct(a.shape, a.dtype) for a in results],
        in_specs=[any_] * 5,
        out_specs=[any_] * 5,
        scratch_shapes=[pltpu.VMEM(a.shape, a.dtype) for a in results] + [dma(5)],
    )(*results)
    return tuple(a.reshape(shape) for a in (proj, dq, dk, dv)) + (dw,)


def solution(mesh):
    tokens, rows = P("fsdp", "frame", None, None), P(("fsdp", "frame"), None)
    return jax.shard_map(
        local,
        mesh=mesh,
        in_specs=(tokens, tokens, tokens, rows, tokens),
        out_specs=(tokens, tokens, tokens, tokens, rows),
        check_vma=False,
    )
```

```python
import functools

import jax
import jax.numpy as jnp
from jax import lax
from jax.experimental import pallas as pl
from jax.experimental.pallas import tpu as pltpu
from jax.sharding import PartitionSpec as P

MESH = pl.DeviceIdType.MESH
F32, BF16 = jnp.float32, jnp.bfloat16
HEAD = 128
ROWS = 256
PART = 64
BAND = 16
WIDTH = 1536
LANES = 512
FACTOR = HEAD ** -0.5
TOKEN_FACTOR = 65536.0 ** -0.5
SETS = ((1, 1, 1, 1), (0, 0, 2, 2), (0, 0, 3, 3))
Q, K, V, G = range(4)
NT = (((1,), (1,)), ((), ()))
TN = (((0,), (0,)), ((), ()))


def dot(a, b, dims=(((1,), (0,)), ((), ()))):
    return lax.dot_general(a, b, dims, preferred_element_type=F32)


def query_blocks(site, where):
    return [b for b in range(4) if where[b] == site]


def key_sites(block, where):
    return [s for s in sorted(set(where)) if block <= max(query_blocks(s, where))]


def lanes_of(s):
    return pl.ds(LANES * s, LANES)


def kernel(q_in, k_in, v_in, w_in, g_in, proj_out, dq_out, dk_out, dv_out, dw_out, *refs):
    refs = list(refs)
    take = lambda n: [refs.pop(0) for _ in range(n)]
    held = [take(4) for _ in SETS]
    attended = take(len(SETS))
    (partial,) = take(1)
    g_home, o_home, ga_home, proj_home = take(4)
    w_slabs, w_pad, w_full = take(3)
    x_own, x_out, x_in, y_out, y_in, z_out, z_in = take(7)
    local_sem, in_send, iy_recv, iz_recv, o_send, o_recv, by_send, home_recv = take(8)
    wz_send, wz_recv, wy_send, wy_recv, wx_send, wx_recv, wc_send, wc_recv = take(8)
    gc_send, gc_recv, oc_send, oc_recv, dx_send, dx_recv, dy_send, dy_recv, dz_send, dz_recv = take(10)

    f = lax.axis_index("fsdp")
    fr = lax.axis_index("frame")
    x, zh, core = f // 4, lax.rem(f // 2, 2), lax.rem(f, 2)
    z, y = fr // 4, lax.rem(fr, 4)
    z8 = zh * 4 + z

    def z_device(d):
        t = lax.rem(z8 + d, 8)
        return {"fsdp": x * 4 + (t // 4) * 2 + core, "frame": lax.rem(t, 4) * 4 + y}

    def y_device(d):
        return {"frame": z * 4 + lax.rem(y + d, 4)}

    def x_device(d):
        return {"fsdp": lax.rem(x + d, 4) * 4 + lax.rem(f, 4)}

    other_core = {"fsdp": f + 1 - 2 * core}

    def remote(src, dst, send, recv, device):
        return pltpu.make_async_remote_copy(
            src_ref=src, dst_ref=dst, send_sem=send, recv_sem=recv, device_id=device, device_id_type=MESH
        )

    def wait_slabs(sem, n):
        if n:
            ref = held[0][0].at[pl.ds(0, n)]
            pltpu.make_async_copy(ref, ref, sem).wait()

    barrier = pltpu.get_barrier_semaphore()
    partners = [{"frame": lax.rem(fr + d, 16)} for d in range(1, 16)]
    partners += [{"fsdp": x * 4 + (1 - zh) * 2 + core, "frame": k * 4 + y} for k in range(4)]
    partners += [x_device(d) for d in (1, 2, 3)] + [other_core]
    for device in partners:
        pl.semaphore_signal(barrier, inc=1, device_id=device, device_id_type=MESH)
    pl.semaphore_wait(barrier, len(partners))

    g_load = pltpu.make_async_copy(g_in, g_home.at[0], local_sem.at[0])
    g_load.start()
    own_rows = pltpu.make_async_copy(w_in, w_slabs.at[y, z8], local_sem.at[1])
    own_rows.start()
    wz = [
        remote(w_in, w_slabs.at[y, z8], wz_send.at[d], wz_recv.at[d], z_device(d)) for d in range(1, 8)
    ]
    for c in wz:
        c.start()

    def at(places, fn, *args):
        for zs in places:
            pl.when(z == zs)(functools.partial(fn, zs, *args))

    every = range(4)
    sent = {}

    def part(ref, j, s):
        return ref.at[pl.ds(pl.multiple_of(j * PART, PART), PART), lanes_of(s)]

    def own(ref, zs):
        return ref.at[pl.ds(4 * zs, 4)]

    def sites_for(b, t, s):
        return [SETS[s][b]] if t in (Q, G) else key_sites(b, SETS[s])

    def others(b, t, s):
        return sorted((a for a in sites_for(b, t, s) if a != b), key=lambda a: -abs(a - b))

    def send_in(zs, t, s):
        src = (q_in, k_in, v_in, ga_home)[t]
        count = 0
        for site in others(zs, t, s) + [zs]:
            if site not in sites_for(zs, t, s):
                continue
            recv = (iy_recv if site == zs else iz_recv).at[t, s]
            for d in (2, 1, 3, 0):
                j = lax.rem(y + d, 4)
                if site == zs and d == 0:
                    pltpu.make_async_copy(part(src, j, s), held[s][t].at[fr], recv).start()
                else:
                    device = {"frame": site * 4 + j}
                    remote(part(src, j, s), held[s][t].at[fr], in_send.at[t, s], recv, device).start()
                    count += 1
        sent["in", zs, t, s] = count

    def wait_in(zs, t, s):
        blocks = query_blocks(zs, SETS[s])
        wait_slabs(iy_recv.at[t, s], 4)
        wait_slabs(iz_recv.at[t, s], 4 * (len(blocks) - 1) if t in (Q, G) else 4 * max(blocks))

    def home(zs, s, b, src, dst, send_sem, recv_sem):
        for d in (2, 1, 3, 0):
            frame = 4 * b + lax.rem(y + d, 4)
            if b == zs and d == 0:
                pltpu.make_async_copy(src.at[frame], dst, recv_sem).start()
            else:
                remote(src.at[frame], dst, send_sem, recv_sem, {"frame": frame}).start()
        return 3 if b == zs else 4

    def geometry(zs, s):
        blocks = query_blocks(zs, SETS[s])
        return 4 * blocks[0], 4 * (blocks[-1] + 1), 4 * (blocks[-1] + 1)

    def bias_of(first, last, keys):
        shape = ((last - first) * BAND, keys * BAND)
        row = lax.broadcasted_iota(jnp.int32, shape, 0)
        col = lax.broadcasted_iota(jnp.int32, shape, 1)
        allowed = ((row & 15) == (col & 15)) & ((row >> 4) + first >= (col >> 4))
        return jnp.where(allowed, 0.0, -jnp.inf).astype(F32)

    def probs_of(queries, keys, bias):
        scores = [dot(a, b, NT) * FACTOR + bias for a, b in zip(queries, keys)]
        top = [jnp.max(a, axis=1, keepdims=True) for a in scores]
        e = [jnp.exp(a - b) for a, b in zip(scores, top)]
        scale = [1.0 / jnp.sum(a, axis=1, keepdims=True) for a in e]
        return [a * b for a, b in zip(e, scale)]

    def heads(fn):
        def step(h, carry):
            fn(pl.ds(pl.multiple_of(h * HEAD, HEAD), HEAD))
            return carry

        lax.fori_loop(0, 4, step, 0)

    bands = [pl.ds(p * BAND, BAND) for p in range(4)]

    def load(ref, a, b, lanes):
        return [ref[a:b, rows, lanes].reshape((b - a) * BAND, HEAD) for rows in bands]

    def store(ref, a, b, lanes, values):
        for rows, value in zip(bands, values):
            ref[a:b, rows, lanes] = value.astype(BF16).reshape(b - a, BAND, HEAD)

    def forward(zs, s):
        first, last, keys = geometry(zs, s)
        for t in (K, V, Q):
            wait_in(zs, t, s)
        bias = bias_of(first, last, keys)

        def head(lanes):
            queries, keys_ = load(held[s][Q], first, last, lanes), load(held[s][K], 0, keys, lanes)
            values = load(held[s][V], 0, keys, lanes)
            weights = [a.astype(BF16) for a in probs_of(queries, keys_, bias)]
            store(attended[s], first, last, lanes, [dot(a, b) for a, b in zip(weights, values)])

        heads(head)
        sent["o", zs, 0, s] = sum(
            home(zs, s, b, attended[s], part(o_home.at[0], y, s), o_send.at[s], o_recv.at[s])
            for b in sorted(query_blocks(zs, SETS[s]), key=lambda b: -abs(b - zs))
        )

    def backward(zs, s):
        first, last, keys = geometry(zs, s)
        wait_in(zs, G, s)
        bias = bias_of(first, last, keys)

        def head(lanes):
            queries, keys_ = load(held[s][Q], first, last, lanes), load(held[s][K], 0, keys, lanes)
            values, grads = load(held[s][V], 0, keys, lanes), load(held[s][G], first, last, lanes)
            grad_probs = [dot(a, b, NT) for a, b in zip(grads, values)]
            probs = probs_of(queries, keys_, bias)
            centre = [jnp.sum(a * b, axis=1, keepdims=True) for a, b in zip(probs, grad_probs)]
            grad_scores = [(a * (b - c)).astype(BF16) for a, b, c in zip(probs, grad_probs, centre)]
            weights = [a.astype(BF16) for a in probs]
            grad_q = [dot(a, b) * FACTOR for a, b in zip(grad_scores, keys_)]
            grad_k = [dot(a, b, TN) * FACTOR for a, b in zip(grad_scores, queries)]
            grad_v = [dot(a, b, TN) for a, b in zip(weights, grads)]
            store(held[s][Q], first, last, lanes, grad_q)
            store(held[s][K], 0, keys, lanes, grad_k)
            store(held[s][V], 0, keys, lanes, grad_v)

        heads(head)
        for t in (K, V):
            give_back(zs, t, s)

    def give_back(zs, t, s):
        blocks = query_blocks(zs, SETS[s]) if t == Q else range(geometry(zs, s)[2] // 4)
        count = 0
        for b in sorted(blocks, key=lambda b: -abs(b - zs)):
            sites = sites_for(b, t, s)
            slot = sites.index(zs)
            dst = (dq_out, dk_out, dv_out)[t]
            dst = part(dst, y, s) if len(sites) == 1 else part(partial.at[t - K, s, slot], y, 0)
            count += home(zs, s, b, held[s][t], dst, by_send.at[t, s], home_recv.at[t, s, slot])
        sent["back", zs, t, s] = count

    def arrived(zs, t, s):
        n = len(sites_for(zs, t, s))
        for slot in range(n):
            wait_slabs(home_recv.at[t, s, slot], 4)
        if n > 1:
            terms = partial.at[t - K, s]

            def add(i, carry):
                rows = pl.ds(pl.multiple_of(i * PART, PART), PART)
                total = terms[0, rows, :].astype(F32)
                for slot in range(1, n):
                    total += terms[slot, rows, :].astype(F32)
                terms[0, rows, :] = total.astype(BF16)
                return carry

            lax.fori_loop(0, ROWS // PART, add, 0)
            dst = (dq_out, dk_out, dv_out)[t]
            pltpu.make_async_copy(terms.at[0], dst.at[:, lanes_of(s)], home_recv.at[t, s, 0]).start()

    def stored(zs, t, s):
        if len(sites_for(zs, t, s)) > 1:
            wait_slabs(home_recv.at[t, s, 0], 4)

    def sites_of(s):
        return sorted(set(SETS[s]))

    g_other = remote(g_in, g_home.at[1], gc_send.at[0], gc_recv.at[0], other_core)
    g_other.start()
    for c in wz:
        c.wait()
    own_rows.wait()
    wy = [
        remote(w_slabs.at[y], w_slabs.at[y], wy_send.at[d], wy_recv.at[d], y_device(d)) for d in (1, 2, 3)
    ]
    for c in wy:
        c.start()

    for s in range(len(SETS)):
        for t in (K, V, Q):
            at(every, send_in, t, s)

    w_pad[...] = jnp.zeros_like(w_pad)
    r = lax.broadcasted_iota(jnp.int32, (96, 128), 0)
    c_ = lax.broadcasted_iota(jnp.int32, (96, 128), 1)
    sixth = (r * 171) >> 10
    pick = jnp.where(c_ == r + 2 * sixth, 1.0, 0.0).astype(BF16)
    for c in wy:
        c.wait()

    def w_rows(xx, h, cc):
        return w_full.at[pl.ds(pl.multiple_of((4 * xx + 2 * h + cc) * 96, 96), 96)]

    def x_from(d):
        return lax.rem(x + 4 - d, 4)

    def core_copy(d, h):
        ref = w_rows(x_from(d), h, core)
        return remote(ref, ref, wc_send.at[d, h], wc_recv.at[d, h], other_core)

    wx = {}
    for h in range(2):
        for i in range(16):
            w_pad[8 * i : 8 * i + 6, :] = w_slabs[i % 4, 4 * h + i // 4].astype(F32)
        w_rows(x, h, core)[...] = dot(pick, w_pad[...].astype(BF16)).astype(BF16)
        for step in (1, 3) if h == 0 else (3, 1):
            ref = w_rows(x, h, core)
            wx[step, h] = remote(ref, ref, wx_send.at[step, h], wx_recv.at[step, h], x_device(step))
            wx[step, h].start()
        core_copy(0, h).start()

    def pass_on(d, h, step=0):
        wx[d, h].wait()
        if step:
            ref = w_rows(x_from(d), h, core)
            wx[2, h] = remote(ref, ref, wx_send.at[2, h], wx_recv.at[2, h], x_device(step))
            wx[2, h].start()
        core_copy(d, h).start()

    pass_on(1, 0, 1)
    pass_on(3, 1, 3)

    at(sites_of(0), forward, 0)
    at(sites_of(1), forward, 1)
    pass_on(1, 1)
    pass_on(3, 0)

    at(sites_of(2), forward, 2)
    pass_on(2, 0)
    pass_on(2, 1)

    def grad_attended(s):
        ga_home[:, lanes_of(s)] = dot(g_home[0], w_full[LANES * s : LANES * (s + 1), :], NT).astype(BF16)
        at(every, send_in, G, s)

    g_load.wait()
    for d in (0, 1, 3):
        for h in range(2):
            core_copy(d, h).wait()
    for side, s in ((x < 2, 0), (x >= 2, 2)):
        pl.when(side)(functools.partial(grad_attended, s))
    for h in range(2):
        core_copy(2, h).wait()
    grad_attended(1)
    for side, s in ((x < 2, 2), (x >= 2, 0)):
        pl.when(side)(functools.partial(grad_attended, s))

    o_other = []
    for s in range(len(SETS)):
        wait_slabs(o_recv.at[s], 4)
        c = remote(
            o_home.at[0, :, lanes_of(s)], o_home.at[1, :, lanes_of(s)], oc_send.at[s], oc_recv.at[s], other_core
        )
        c.start()
        o_other.append(c)

    g_other.wait()
    for c in o_other:
        c.wait()
    r = lax.broadcasted_iota(jnp.int32, (384, 192), 0)
    c_ = lax.broadcasted_iota(jnp.int32, (384, 192), 1)
    side = jnp.where(r == c_ + 96 * core + jnp.where(c_ >= 96, 96, 0), 1.0, 0.0).astype(BF16)
    dx = {}
    for d in (2, 1, 3, 0):
        block = pl.ds(pl.multiple_of(lax.rem(x + d, 4) * 384, 384), 384)
        left = dot(o_home[:, :, block].reshape(2 * ROWS, 384), side).astype(BF16)
        for n in range(3):
            cols = pl.ds(n * LANES, LANES)
            term = dot(left, g_home[:, :, cols].reshape(2 * ROWS, LANES), TN) * TOKEN_FACTOR
            if d:
                x_out[d, :, cols] = term.astype(BF16)
            else:
                x_own[:, cols] = term
        if d:
            dx[d] = remote(x_out.at[d], x_in.at[d], dx_send.at[d], dx_recv.at[d], x_device(d))
            dx[d].start()

    for s in range(len(SETS)):
        at(sites_of(s), backward, s)

    for n in range(3):
        cols = pl.ds(n * LANES, LANES)
        proj_home[:, cols] = dot(o_home[0], w_full[:, cols]).astype(BF16)
    proj_copy = pltpu.make_async_copy(proj_home, proj_out, local_sem.at[2])
    proj_copy.start()

    for d in (1, 2, 3):
        dx[d].wait()
    r = lax.broadcasted_iota(jnp.int32, (192, 192), 0)
    c_ = lax.broadcasted_iota(jnp.int32, (192, 192), 1)
    slab = (r * 171) >> 10
    source = 24 * (slab & 7) + 6 * (slab >> 3) + (r - 6 * slab)
    order = jnp.where(c_ == source, 1.0, 0.0).astype(BF16)
    for n in range(3):
        cols = pl.ds(n * LANES, LANES)
        total = x_own[:, cols]
        for d in (1, 2, 3):
            total += x_in[d, :, cols].astype(F32)
        y_out[:, :, cols] = dot(order, total.astype(BF16)).astype(BF16).reshape(4, 48, LANES)
    dy = {}
    for d in (1, 2, 3):
        dy[d] = remote(y_out.at[lax.rem(y + d, 4)], y_in.at[d], dy_send.at[d], dy_recv.at[d], y_device(d))
        dy[d].start()

    for d in (1, 2, 3):
        dy[d].wait()
    r = lax.broadcasted_iota(jnp.int32, (64, 48), 0)
    c_ = lax.broadcasted_iota(jnp.int32, (64, 48), 1)
    apart = jnp.where((c_ == r - 2 * (r >> 3)) & ((r & 7) < 6), 1.0, 0.0).astype(BF16)
    total = y_out[y].astype(F32)
    for d in (1, 2, 3):
        total += y_in[d].astype(F32)
    slabs = dot(apart, total.astype(BF16))
    for i in range(8):
        z_out[i] = slabs[8 * i : 8 * i + 6].astype(BF16)
    dz = {}
    for d in range(1, 8):
        dz[d] = remote(z_out.at[lax.rem(z8 + d, 8)], z_in.at[d], dz_send.at[d], dz_recv.at[d], z_device(d))
        dz[d].start()

    for s in range(len(SETS)):
        at(sites_of(s), give_back, Q, s)
    for s in range(len(SETS)):
        for t in (K, V, Q):
            at(every, arrived, t, s)

    for d in range(1, 8):
        dz[d].wait()
    total = z_out[z8].astype(F32)
    for d in range(1, 8):
        total += z_in[d].astype(F32)
    dw_out[...] = total

    proj_copy.wait()

    def drain(zs):
        for s in range(len(SETS)):
            for t in range(4):
                wait_slabs(in_send.at[t, s], sent["in", zs, t, s])
            for t in (K, V, Q):
                stored(zs, t, s)
            if zs in SETS[s]:
                wait_slabs(o_send.at[s], sent["o", zs, 0, s])
                for t in (K, V, Q):
                    wait_slabs(by_send.at[t, s], sent["back", zs, t, s])

    at(every, drain)


def hand_on(*refs):
    n = len(refs) // 3
    sources, results, held, sem = refs[:n], refs[n : 2 * n], refs[2 * n : 3 * n], refs[3 * n]
    loads = [pltpu.make_async_copy(a, b, sem.at[i]) for i, (a, b) in enumerate(zip(sources, held))]
    stores = [pltpu.make_async_copy(a, b, sem.at[i]) for i, (a, b) in enumerate(zip(held, results))]
    for c in loads:
        c.start()
    for c, d in zip(loads, stores):
        c.wait()
        d.start()
    for c in stores:
        c.wait()


def local(queries, key_vectors, value_vectors, out_weight, grad_out):
    shape = queries.shape
    flat = lambda a: a.reshape(ROWS, WIDTH)
    any_, vmem = pl.BlockSpec(memory_space=pl.ANY), pl.BlockSpec(memory_space=pltpu.VMEM)
    dma = lambda *n: pltpu.SemaphoreType.DMA(n)
    n = len(SETS)
    big = jax.ShapeDtypeStruct((ROWS, WIDTH), BF16)
    scratch = [pltpu.VMEM((16, PART, LANES), BF16)] * (5 * n)
    scratch += [pltpu.VMEM((2, n, 2, ROWS, LANES), BF16)]
    scratch += [pltpu.VMEM((2, ROWS, WIDTH), BF16)] * 2 + [pltpu.VMEM((ROWS, WIDTH), BF16)] * 2
    scratch += [pltpu.VMEM((4, 8, 6, WIDTH), BF16), pltpu.VMEM((128, WIDTH), F32), pltpu.VMEM((WIDTH, WIDTH), BF16)]
    scratch += [
        pltpu.VMEM((192, WIDTH), F32),
        pltpu.VMEM((4, 192, WIDTH), BF16),
        pltpu.VMEM((4, 192, WIDTH), BF16),
        pltpu.VMEM((4, 48, WIDTH), BF16),
        pltpu.VMEM((4, 48, WIDTH), BF16),
        pltpu.VMEM((8, 6, WIDTH), BF16),
        pltpu.VMEM((8, 6, WIDTH), BF16),
    ]
    scratch += [dma(3), dma(4, n), dma(4, n), dma(4, n)]
    scratch += [dma(n), dma(n), dma(3, n), dma(3, n, 2)]
    scratch += [dma(8), dma(8), dma(4), dma(4), dma(4, 2), dma(4, 2), dma(4, 2), dma(4, 2)]
    scratch += [dma(1), dma(1), dma(n), dma(n), dma(4), dma(4), dma(4), dma(4), dma(8), dma(8)]
    proj, dq, dk, dv, dw = pl.pallas_call(
        kernel,
        out_shape=[big] * 4 + [jax.ShapeDtypeStruct((6, WIDTH), F32)],
        in_specs=[any_] * 5,
        out_specs=[any_] * 4 + [vmem],
        scratch_shapes=scratch,
        compiler_params=pltpu.CompilerParams(
            collective_id=0, has_side_effects=True, vmem_limit_bytes=63 * 2**20
        ),
    )(flat(queries), flat(key_vectors), flat(value_vectors), out_weight, flat(grad_out))
    results = (proj, dq, dk, dv, dw)
    proj, dq, dk, dv, dw = pl.pallas_call(
        hand_on,
        out_shape=[jax.ShapeDtypeStruct(a.shape, a.dtype) for a in results],
        in_specs=[any_] * 5,
        out_specs=[any_] * 5,
        scratch_shapes=[pltpu.VMEM(a.shape, a.dtype) for a in results] + [dma(5)],
    )(*results)
    return tuple(a.reshape(shape) for a in (proj, dq, dk, dv)) + (dw,)


def solution(mesh):
    tokens, rows = P("fsdp", "frame", None, None), P(("fsdp", "frame"), None)
    return jax.shard_map(
        local,
        mesh=mesh,
        in_specs=(tokens, tokens, tokens, rows, tokens),
        out_specs=(tokens, tokens, tokens, tokens, rows),
        check_vma=False,
    )
```

```python
import functools

import jax
import jax.numpy as jnp
from jax import lax
from jax.experimental import pallas as pl
from jax.experimental.pallas import tpu as pltpu
from jax.sharding import PartitionSpec as P

MESH = pl.DeviceIdType.MESH
F32, BF16 = jnp.float32, jnp.bfloat16
HEAD = 128
ROWS = 256
PART = 64
BAND = 16
WIDTH = 1536
LANES = 512
FACTOR = HEAD ** -0.5
TOKEN_FACTOR = 65536.0 ** -0.5
SETS = ((1, 1, 1, 1), (0, 0, 2, 2), (0, 0, 3, 3))
Q, K, V, G = range(4)
NT = (((1,), (1,)), ((), ()))
TN = (((0,), (0,)), ((), ()))


def dot(a, b, dims=(((1,), (0,)), ((), ()))):
    return lax.dot_general(a, b, dims, preferred_element_type=F32)


def query_blocks(site, where):
    return [b for b in range(4) if where[b] == site]


def key_sites(block, where):
    return [s for s in sorted(set(where)) if block <= max(query_blocks(s, where))]


def lanes_of(s):
    return pl.ds(LANES * s, LANES)


def kernel(q_in, k_in, v_in, w_in, g_in, proj_out, dq_out, dk_out, dv_out, dw_out, *refs):
    refs = list(refs)
    take = lambda n: [refs.pop(0) for _ in range(n)]
    held = [take(4) for _ in SETS]
    attended = take(len(SETS))
    (partial,) = take(1)
    g_home, o_home, ga_home, proj_home = take(4)
    w_slabs, w_pad, w_full = take(3)
    x_own, x_out, x_in, y_out, y_in, z_out, z_in = take(7)
    local_sem, in_send, iy_recv, iz_recv, o_send, o_recv, by_send, home_recv = take(8)
    wz_send, wz_recv, wy_send, wy_recv, wx_send, wx_recv, wc_send, wc_recv = take(8)
    gc_send, gc_recv, oc_send, oc_recv, dx_send, dx_recv, dy_send, dy_recv, dz_send, dz_recv = take(10)

    f = lax.axis_index("fsdp")
    fr = lax.axis_index("frame")
    x, zh, core = f // 4, lax.rem(f // 2, 2), lax.rem(f, 2)
    z, y = fr // 4, lax.rem(fr, 4)
    z8 = zh * 4 + z

    def z_device(d):
        t = lax.rem(z8 + d, 8)
        return {"fsdp": x * 4 + (t // 4) * 2 + core, "frame": lax.rem(t, 4) * 4 + y}

    def y_device(d):
        return {"frame": z * 4 + lax.rem(y + d, 4)}

    def x_device(d):
        return {"fsdp": lax.rem(x + d, 4) * 4 + lax.rem(f, 4)}

    other_core = {"fsdp": f + 1 - 2 * core}

    def remote(src, dst, send, recv, device):
        return pltpu.make_async_remote_copy(
            src_ref=src, dst_ref=dst, send_sem=send, recv_sem=recv, device_id=device, device_id_type=MESH
        )

    def wait_slabs(sem, n):
        if n:
            ref = held[0][0].at[pl.ds(0, n)]
            pltpu.make_async_copy(ref, ref, sem).wait()

    barrier = pltpu.get_barrier_semaphore()
    partners = [{"frame": lax.rem(fr + d, 16)} for d in range(1, 16)]
    partners += [{"fsdp": x * 4 + (1 - zh) * 2 + core, "frame": k * 4 + y} for k in range(4)]
    partners += [x_device(d) for d in (1, 2, 3)] + [other_core]
    for device in partners:
        pl.semaphore_signal(barrier, inc=1, device_id=device, device_id_type=MESH)
    pl.semaphore_wait(barrier, len(partners))

    g_load = pltpu.make_async_copy(g_in, g_home.at[0], local_sem.at[0])
    g_load.start()
    own_rows = pltpu.make_async_copy(w_in, w_slabs.at[y, z8], local_sem.at[1])
    own_rows.start()
    wz = [
        remote(w_in, w_slabs.at[y, z8], wz_send.at[d], wz_recv.at[d], z_device(d)) for d in range(1, 8)
    ]
    for c in wz:
        c.start()

    def at(places, fn, *args):
        for zs in places:
            pl.when(z == zs)(functools.partial(fn, zs, *args))

    every = range(4)
    sent = {}

    def part(ref, j, s):
        return ref.at[pl.ds(pl.multiple_of(j * PART, PART), PART), lanes_of(s)]

    def own(ref, zs):
        return ref.at[pl.ds(4 * zs, 4)]

    def sites_for(b, t, s):
        return [SETS[s][b]] if t in (Q, G) else key_sites(b, SETS[s])

    def others(b, t, s):
        return sorted((a for a in sites_for(b, t, s) if a != b), key=lambda a: -abs(a - b))

    def send_in(zs, t, s):
        src = (q_in, k_in, v_in, ga_home)[t]
        count = 0
        for site in others(zs, t, s) + [zs]:
            if site not in sites_for(zs, t, s):
                continue
            recv = (iy_recv if site == zs else iz_recv).at[t, s]
            for d in (2, 1, 3, 0):
                j = lax.rem(y + d, 4)
                if site == zs and d == 0:
                    pltpu.make_async_copy(part(src, j, s), held[s][t].at[fr], recv).start()
                else:
                    device = {"frame": site * 4 + j}
                    remote(part(src, j, s), held[s][t].at[fr], in_send.at[t, s], recv, device).start()
                    count += 1
        sent["in", zs, t, s] = count

    def wait_in(zs, t, s):
        blocks = query_blocks(zs, SETS[s])
        wait_slabs(iy_recv.at[t, s], 4)
        wait_slabs(iz_recv.at[t, s], 4 * (len(blocks) - 1) if t in (Q, G) else 4 * max(blocks))

    def home(zs, s, b, src, dst, send_sem, recv_sem):
        for d in (2, 1, 3, 0):
            frame = 4 * b + lax.rem(y + d, 4)
            if b == zs and d == 0:
                pltpu.make_async_copy(src.at[frame], dst, recv_sem).start()
            else:
                remote(src.at[frame], dst, send_sem, recv_sem, {"frame": frame}).start()
        return 3 if b == zs else 4

    def geometry(zs, s):
        blocks = query_blocks(zs, SETS[s])
        return 4 * blocks[0], 4 * (blocks[-1] + 1), 4 * (blocks[-1] + 1)

    def bias_of(first, last, keys):
        shape = ((last - first) * BAND, keys * BAND)
        row = lax.broadcasted_iota(jnp.int32, shape, 0)
        col = lax.broadcasted_iota(jnp.int32, shape, 1)
        allowed = ((row & 15) == (col & 15)) & ((row >> 4) + first >= (col >> 4))
        return jnp.where(allowed, 0.0, -jnp.inf).astype(F32)

    def probs_of(queries, keys, bias):
        scores = [dot(a, b, NT) * FACTOR + bias for a, b in zip(queries, keys)]
        top = [jnp.max(a, axis=1, keepdims=True) for a in scores]
        e = [jnp.exp(a - b) for a, b in zip(scores, top)]
        scale = [1.0 / jnp.sum(a, axis=1, keepdims=True) for a in e]
        return [a * b for a, b in zip(e, scale)]

    def heads(fn):
        def step(h, carry):
            fn(pl.ds(pl.multiple_of(h * HEAD, HEAD), HEAD))
            return carry

        lax.fori_loop(0, 4, step, 0)

    bands = [pl.ds(p * BAND, BAND) for p in range(4)]

    def load(ref, a, b, lanes):
        return [ref[a:b, rows, lanes].reshape((b - a) * BAND, HEAD) for rows in bands]

    def store(ref, a, b, lanes, values):
        for rows, value in zip(bands, values):
            ref[a:b, rows, lanes] = value.astype(BF16).reshape(b - a, BAND, HEAD)

    def forward(zs, s):
        first, last, keys = geometry(zs, s)
        for t in (K, V, Q):
            wait_in(zs, t, s)
        bias = bias_of(first, last, keys)

        def head(lanes):
            queries, keys_ = load(held[s][Q], first, last, lanes), load(held[s][K], 0, keys, lanes)
            values = load(held[s][V], 0, keys, lanes)
            weights = [a.astype(BF16) for a in probs_of(queries, keys_, bias)]
            store(attended[s], first, last, lanes, [dot(a, b) for a, b in zip(weights, values)])

        heads(head)
        sent["o", zs, 0, s] = sum(
            home(zs, s, b, attended[s], part(o_home.at[0], y, s), o_send.at[s], o_recv.at[s])
            for b in sorted(query_blocks(zs, SETS[s]), key=lambda b: -abs(b - zs))
        )

    def backward(zs, s):
        first, last, keys = geometry(zs, s)
        wait_in(zs, G, s)
        bias = bias_of(first, last, keys)

        def head(lanes):
            queries, keys_ = load(held[s][Q], first, last, lanes), load(held[s][K], 0, keys, lanes)
            values, grads = load(held[s][V], 0, keys, lanes), load(held[s][G], first, last, lanes)
            grad_probs = [dot(a, b, NT) for a, b in zip(grads, values)]
            probs = probs_of(queries, keys_, bias)
            centre = [jnp.sum(a * b, axis=1, keepdims=True) for a, b in zip(probs, grad_probs)]
            grad_scores = [(a * (b - c)).astype(BF16) for a, b, c in zip(probs, grad_probs, centre)]
            weights = [a.astype(BF16) for a in probs]
            grad_q = [dot(a, b) * FACTOR for a, b in zip(grad_scores, keys_)]
            grad_k = [dot(a, b, TN) * FACTOR for a, b in zip(grad_scores, queries)]
            grad_v = [dot(a, b, TN) for a, b in zip(weights, grads)]
            store(held[s][Q], first, last, lanes, grad_q)
            store(held[s][K], 0, keys, lanes, grad_k)
            store(held[s][V], 0, keys, lanes, grad_v)

        heads(head)
        for t in (K, V):
            give_back(zs, t, s)

    def give_back(zs, t, s):
        blocks = query_blocks(zs, SETS[s]) if t == Q else range(geometry(zs, s)[2] // 4)
        count = 0
        for b in sorted(blocks, key=lambda b: -abs(b - zs)):
            sites = sites_for(b, t, s)
            slot = sites.index(zs)
            dst = (dq_out, dk_out, dv_out)[t]
            dst = part(dst, y, s) if len(sites) == 1 else part(partial.at[t - K, s, slot], y, 0)
            count += home(zs, s, b, held[s][t], dst, by_send.at[t, s], home_recv.at[t, s, slot])
        sent["back", zs, t, s] = count

    def arrived(zs, t, s):
        n = len(sites_for(zs, t, s))
        for slot in range(n):
            wait_slabs(home_recv.at[t, s, slot], 4)
        if n > 1:
            terms = partial.at[t - K, s]

            def add(i, carry):
                rows = pl.ds(pl.multiple_of(i * PART, PART), PART)
                total = terms[0, rows, :].astype(F32)
                for slot in range(1, n):
                    total += terms[slot, rows, :].astype(F32)
                terms[0, rows, :] = total.astype(BF16)
                return carry

            lax.fori_loop(0, ROWS // PART, add, 0)
            dst = (dq_out, dk_out, dv_out)[t]
            pltpu.make_async_copy(terms.at[0], dst.at[:, lanes_of(s)], home_recv.at[t, s, 0]).start()

    def stored(zs, t, s):
        if len(sites_for(zs, t, s)) > 1:
            wait_slabs(home_recv.at[t, s, 0], 4)

    def sites_of(s):
        return sorted(set(SETS[s]))

    g_other = remote(g_in, g_home.at[1], gc_send.at[0], gc_recv.at[0], other_core)
    g_other.start()
    for c in wz:
        c.wait()
    own_rows.wait()
    wy = [
        remote(w_slabs.at[y], w_slabs.at[y], wy_send.at[d], wy_recv.at[d], y_device(d)) for d in (1, 2, 3)
    ]
    for c in wy:
        c.start()

    for s in range(len(SETS)):
        for t in (K, V, Q):
            at(every, send_in, t, s)

    w_pad[...] = jnp.zeros_like(w_pad)
    r = lax.broadcasted_iota(jnp.int32, (96, 128), 0)
    c_ = lax.broadcasted_iota(jnp.int32, (96, 128), 1)
    sixth = (r * 171) >> 10
    pick = jnp.where(c_ == r + 2 * sixth, 1.0, 0.0).astype(BF16)
    for c in wy:
        c.wait()

    def w_rows(xx, h, cc):
        return w_full.at[pl.ds(pl.multiple_of((4 * xx + 2 * h + cc) * 96, 96), 96)]

    def x_from(d):
        return lax.rem(x + 4 - d, 4)

    def core_copy(d, h):
        ref = w_rows(x_from(d), h, core)
        return remote(ref, ref, wc_send.at[d, h], wc_recv.at[d, h], other_core)

    wx = {}
    for h in range(2):
        for i in range(16):
            w_pad[8 * i : 8 * i + 6, :] = w_slabs[i % 4, 4 * h + i // 4].astype(F32)
        w_rows(x, h, core)[...] = dot(pick, w_pad[...].astype(BF16)).astype(BF16)
        for step in (1, 3) if h == 0 else (3, 1):
            ref = w_rows(x, h, core)
            wx[step, h] = remote(ref, ref, wx_send.at[step, h], wx_recv.at[step, h], x_device(step))
            wx[step, h].start()
        core_copy(0, h).start()

    def pass_on(d, h, step=0):
        wx[d, h].wait()
        if step:
            ref = w_rows(x_from(d), h, core)
            wx[2, h] = remote(ref, ref, wx_send.at[2, h], wx_recv.at[2, h], x_device(step))
            wx[2, h].start()
        core_copy(d, h).start()

    pass_on(1, 0, 1)
    pass_on(3, 1, 3)

    at(sites_of(0), forward, 0)
    at(sites_of(1), forward, 1)
    pass_on(1, 1)
    pass_on(3, 0)

    at(sites_of(2), forward, 2)
    pass_on(2, 0)
    pass_on(2, 1)

    def grad_attended(s):
        ga_home[:, lanes_of(s)] = dot(g_home[0], w_full[LANES * s : LANES * (s + 1), :], NT).astype(BF16)
        at(every, send_in, G, s)

    g_load.wait()
    for d in (0, 1, 3):
        for h in range(2):
            core_copy(d, h).wait()
    for side, s in ((x < 2, 0), (x >= 2, 2)):
        pl.when(side)(functools.partial(grad_attended, s))
    for h in range(2):
        core_copy(2, h).wait()
    grad_attended(1)
    for side, s in ((x < 2, 2), (x >= 2, 0)):
        pl.when(side)(functools.partial(grad_attended, s))

    o_other = []
    for s in range(len(SETS)):
        wait_slabs(o_recv.at[s], 4)
        c = remote(
            o_home.at[0, :, lanes_of(s)], o_home.at[1, :, lanes_of(s)], oc_send.at[s], oc_recv.at[s], other_core
        )
        c.start()
        o_other.append(c)

    g_other.wait()
    for c in o_other:
        c.wait()
    r = lax.broadcasted_iota(jnp.int32, (384, 192), 0)
    c_ = lax.broadcasted_iota(jnp.int32, (384, 192), 1)
    side = jnp.where(r == c_ + 96 * core + jnp.where(c_ >= 96, 96, 0), 1.0, 0.0).astype(BF16)
    dx = {}
    for d in (2, 1, 3, 0):
        block = pl.ds(pl.multiple_of(lax.rem(x + d, 4) * 384, 384), 384)
        left = dot(o_home[:, :, block].reshape(2 * ROWS, 384), side).astype(BF16)
        for n in range(3):
            cols = pl.ds(n * LANES, LANES)
            term = dot(left, g_home[:, :, cols].reshape(2 * ROWS, LANES), TN) * TOKEN_FACTOR
            if d:
                x_out[d, :, cols] = term.astype(BF16)
            else:
                x_own[:, cols] = term
        if d:
            dx[d] = remote(x_out.at[d], x_in.at[d], dx_send.at[d], dx_recv.at[d], x_device(d))
            dx[d].start()

    for s in range(len(SETS)):
        at(sites_of(s), backward, s)

    for d in (1, 2, 3):
        dx[d].wait()
    r = lax.broadcasted_iota(jnp.int32, (192, 192), 0)
    c_ = lax.broadcasted_iota(jnp.int32, (192, 192), 1)
    slab = (r * 171) >> 10
    source = 24 * (slab & 7) + 6 * (slab >> 3) + (r - 6 * slab)
    order = jnp.where(c_ == source, 1.0, 0.0).astype(BF16)
    for n in range(3):
        cols = pl.ds(n * LANES, LANES)
        total = x_own[:, cols]
        for d in (1, 2, 3):
            total += x_in[d, :, cols].astype(F32)
        y_out[:, :, cols] = dot(order, total.astype(BF16)).astype(BF16).reshape(4, 48, LANES)
    dy = {}
    for d in (1, 2, 3):
        dy[d] = remote(y_out.at[lax.rem(y + d, 4)], y_in.at[d], dy_send.at[d], dy_recv.at[d], y_device(d))
        dy[d].start()

    for n in range(3):
        cols = pl.ds(n * LANES, LANES)
        proj_home[:, cols] = dot(o_home[0], w_full[:, cols]).astype(BF16)
    proj_copy = pltpu.make_async_copy(proj_home, proj_out, local_sem.at[2])
    proj_copy.start()

    for d in (1, 2, 3):
        dy[d].wait()
    r = lax.broadcasted_iota(jnp.int32, (64, 48), 0)
    c_ = lax.broadcasted_iota(jnp.int32, (64, 48), 1)
    apart = jnp.where((c_ == r - 2 * (r >> 3)) & ((r & 7) < 6), 1.0, 0.0).astype(BF16)
    total = y_out[y].astype(F32)
    for d in (1, 2, 3):
        total += y_in[d].astype(F32)
    slabs = dot(apart, total.astype(BF16))
    for i in range(8):
        z_out[i] = slabs[8 * i : 8 * i + 6].astype(BF16)
    dz = {}
    for d in range(1, 8):
        dz[d] = remote(z_out.at[lax.rem(z8 + d, 8)], z_in.at[d], dz_send.at[d], dz_recv.at[d], z_device(d))
        dz[d].start()

    for s in range(len(SETS)):
        at(sites_of(s), give_back, Q, s)
    for s in range(len(SETS)):
        for t in (K, V, Q):
            at(every, arrived, t, s)

    for d in range(1, 8):
        dz[d].wait()
    total = z_out[z8].astype(F32)
    for d in range(1, 8):
        total += z_in[d].astype(F32)
    dw_out[...] = total

    proj_copy.wait()

    def drain(zs):
        for s in range(len(SETS)):
            for t in range(4):
                wait_slabs(in_send.at[t, s], sent["in", zs, t, s])
            for t in (K, V, Q):
                stored(zs, t, s)
            if zs in SETS[s]:
                wait_slabs(o_send.at[s], sent["o", zs, 0, s])
                for t in (K, V, Q):
                    wait_slabs(by_send.at[t, s], sent["back", zs, t, s])

    at(every, drain)


def hand_on(*refs):
    n = len(refs) // 3
    sources, results, held, sem = refs[:n], refs[n : 2 * n], refs[2 * n : 3 * n], refs[3 * n]
    loads = [pltpu.make_async_copy(a, b, sem.at[i]) for i, (a, b) in enumerate(zip(sources, held))]
    stores = [pltpu.make_async_copy(a, b, sem.at[i]) for i, (a, b) in enumerate(zip(held, results))]
    for c in loads:
        c.start()
    for c, d in zip(loads, stores):
        c.wait()
        d.start()
    for c in stores:
        c.wait()


def local(queries, key_vectors, value_vectors, out_weight, grad_out):
    shape = queries.shape
    flat = lambda a: a.reshape(ROWS, WIDTH)
    any_, vmem = pl.BlockSpec(memory_space=pl.ANY), pl.BlockSpec(memory_space=pltpu.VMEM)
    dma = lambda *n: pltpu.SemaphoreType.DMA(n)
    n = len(SETS)
    big = jax.ShapeDtypeStruct((ROWS, WIDTH), BF16)
    scratch = [pltpu.VMEM((16, PART, LANES), BF16)] * (5 * n)
    scratch += [pltpu.VMEM((2, n, 2, ROWS, LANES), BF16)]
    scratch += [pltpu.VMEM((2, ROWS, WIDTH), BF16)] * 2 + [pltpu.VMEM((ROWS, WIDTH), BF16)] * 2
    scratch += [pltpu.VMEM((4, 8, 6, WIDTH), BF16), pltpu.VMEM((128, WIDTH), F32), pltpu.VMEM((WIDTH, WIDTH), BF16)]
    scratch += [
        pltpu.VMEM((192, WIDTH), F32),
        pltpu.VMEM((4, 192, WIDTH), BF16),
        pltpu.VMEM((4, 192, WIDTH), BF16),
        pltpu.VMEM((4, 48, WIDTH), BF16),
        pltpu.VMEM((4, 48, WIDTH), BF16),
        pltpu.VMEM((8, 6, WIDTH), BF16),
        pltpu.VMEM((8, 6, WIDTH), BF16),
    ]
    scratch += [dma(3), dma(4, n), dma(4, n), dma(4, n)]
    scratch += [dma(n), dma(n), dma(3, n), dma(3, n, 2)]
    scratch += [dma(8), dma(8), dma(4), dma(4), dma(4, 2), dma(4, 2), dma(4, 2), dma(4, 2)]
    scratch += [dma(1), dma(1), dma(n), dma(n), dma(4), dma(4), dma(4), dma(4), dma(8), dma(8)]
    proj, dq, dk, dv, dw = pl.pallas_call(
        kernel,
        out_shape=[big] * 4 + [jax.ShapeDtypeStruct((6, WIDTH), F32)],
        in_specs=[any_] * 5,
        out_specs=[any_] * 4 + [vmem],
        scratch_shapes=scratch,
        compiler_params=pltpu.CompilerParams(
            collective_id=0, has_side_effects=True, vmem_limit_bytes=63 * 2**20
        ),
    )(flat(queries), flat(key_vectors), flat(value_vectors), out_weight, flat(grad_out))
    results = (proj, dq, dk, dv, dw)
    proj, dq, dk, dv, dw = pl.pallas_call(
        hand_on,
        out_shape=[jax.ShapeDtypeStruct(a.shape, a.dtype) for a in results],
        in_specs=[any_] * 5,
        out_specs=[any_] * 5,
        scratch_shapes=[pltpu.VMEM(a.shape, a.dtype) for a in results] + [dma(5)],
    )(*results)
    return tuple(a.reshape(shape) for a in (proj, dq, dk, dv)) + (dw,)


def solution(mesh):
    tokens, rows = P("fsdp", "frame", None, None), P(("fsdp", "frame"), None)
    return jax.shard_map(
        local,
        mesh=mesh,
        in_specs=(tokens, tokens, tokens, rows, tokens),
        out_specs=(tokens, tokens, tokens, tokens, rows),
        check_vma=False,
    )
```
